128 devices in a mesh: dp: 8 (over z, core), tensor: 16 (over y, x).
Axes of the slice: x: 4, y: 4, z: 4, core: 2. Of those that a mesh axis runs over, the one named last changes fastest.
Arguments:
- tokens: bfloat16 [1280, 8192], P('tensor', 'dp'), may hold values from -6 to 6
- gate_weight: bfloat16 [8192, 14336], P('dp', 'tensor'), may hold values from -0.1875 to 0.1875
- up_weight: bfloat16 [8192, 14336], P('dp', 'tensor'), may hold values from -0.1875 to 0.1875
- down_weight: bfloat16 [14336, 8192], P('tensor', 'dp'), may hold values from -0.046875 to 0.046875
- d_mixed: bfloat16 [1280, 8192], P('tensor', 'dp'), may hold values from -1.5 to 1.5
Outputs:
- mixed: bfloat16 [1280, 8192], P('tensor', 'dp')
- d_tokens: bfloat16 [1280, 8192], P('tensor', 'dp')
- grad_gate: float32 [8192, 14336], P('dp', 'tensor')
- grad_up: float32 [8192, 14336], P('dp', 'tensor')
- grad_down: float32 [14336, 8192], P('tensor', 'dp')
The draws below stay inside these ranges and needn't reach their ends.
All inputs are finite; a program needn't handle non-finite values. Where the reference program divides by a largest or mean magnitude, that divisor is 1e-20 or more.
Results may differ from the reference program's by a relative error of at most 0.0063.
Values may be sent and summed in bfloat16 or wider, within the bound.
No kernel may reach another device: no remote copies, remote signals or barrier semaphores. Data moves between devices by JAX's collectives and lax.ppermute only.
A program may use at most 128 MiB of HBM per device.

```python
import math
import jax
import jax.numpy as jnp
import numpy as np
from jax import lax

D = 8192
FF = 14336
BLOCK = 128
TOKENS = 1280


def levels(rng, dims, shards, smallest, largest):
    gain = 1.0
    for dim, shards_of in shards:
        heights = jax.random.uniform(jax.random.fold_in(jax.random.fold_in(rng, 6), dim), (shards_of,), jnp.float32, smallest / len(shards), largest / len(shards))
        gain = gain * jnp.repeat(jnp.exp(heights), dims[dim] // shards_of).reshape((-1,) + (1,) * (len(dims) - 1 - dim))
    return gain


def scatter_about(key, shape, spread, reach, pieces=(), dtype=jnp.bfloat16):
    result = jax.random.normal(key, shape, jnp.float32) * spread
    if len(pieces) > 0:
        result = levels(key, shape, pieces, -0.22, 0.18) * result
    return jnp.clip(result, min=-reach, max=reach).astype(dtype)


def setup_inputs(seed: int = 0) -> dict:
    arg_keys = jax.random.split(jax.random.key(seed), 6)
    tokens = scatter_about(arg_keys[0], (TOKENS, D), 1.0, 6.0, ((0, 16), (1, 8)))
    gate_weight = scatter_about(arg_keys[1], (D, FF), (D // 8) ** -0.5, 0.1875, ((0, 8), (1, 16)))
    up_weight = scatter_about(arg_keys[2], (D, FF), (D // 8) ** -0.5, 0.1875, ((0, 8), (1, 16)))
    down_weight = scatter_about(arg_keys[3], (FF, D), FF ** -0.5, 0.046875, ((0, 16), (1, 8)))
    d_mixed = scatter_about(arg_keys[4], (TOKENS, D), 0.25, 1.5, ((0, 16), (1, 8)))
    return {"tokens": tokens, "gate_weight": gate_weight, "up_weight": up_weight, "down_weight": down_weight, "d_mixed": d_mixed}


def hadamard(order):
    index = np.arange(order)
    matrix = np.ones((order, order))
    for bit_index in range(max(order.bit_length() - 1, 0)):
        both = (index[:, None] >> bit_index & 1) * (index[None, :] >> bit_index & 1)
        matrix = matrix * (1 - 2 * both)
    return jnp.asarray(matrix, jnp.float32)

def rotate_rows(values):
    hadamard_table = hadamard(BLOCK)
    turned = jnp.einsum('tkc,kj->tjc', values, hadamard_table, precision=lax.Precision.HIGHEST)
    return turned / math.sqrt(BLOCK)

def reference(tokens, gate_weight, up_weight, down_weight, d_mixed):
    groups = D // BLOCK
    rotated = rotate_rows(tokens.astype(jnp.float32).reshape(TOKENS, BLOCK, groups))
    block_scale = lax.optimization_barrier(jnp.max(jnp.abs(rotated), axis=1, keepdims=True)) + 1e-05
    scaled = (rotated / block_scale).astype(jnp.bfloat16).reshape(TOKENS, D)
    gate_all = jnp.dot(scaled, gate_weight, preferred_element_type=jnp.float32)
    up_all = jnp.dot(scaled, up_weight, preferred_element_type=jnp.float32)
    sigmoid_gate = jax.nn.sigmoid(gate_all)
    silu_gate = gate_all * sigmoid_gate
    hidden = (silu_gate * up_all).astype(jnp.bfloat16)
    mixed = jnp.dot(hidden, down_weight, preferred_element_type=jnp.float32).astype(jnp.bfloat16)
    hidden_grad = jnp.dot(d_mixed, down_weight.T, preferred_element_type=jnp.float32)
    grad_down = jnp.dot(hidden.T, d_mixed, preferred_element_type=jnp.float32)
    gate_grad = (hidden_grad * up_all * sigmoid_gate * (1.0 + gate_all * (1.0 - sigmoid_gate))).astype(jnp.bfloat16)
    up_grad = (hidden_grad * silu_gate).astype(jnp.bfloat16)
    grad_gate = jnp.dot(scaled.T, gate_grad, preferred_element_type=jnp.float32)
    grad_up = jnp.dot(scaled.T, up_grad, preferred_element_type=jnp.float32)
    scaled_grad = jnp.dot(gate_grad, gate_weight.T, preferred_element_type=jnp.float32)
    scaled_grad = scaled_grad + jnp.dot(up_grad, up_weight.T, preferred_element_type=jnp.float32)
    unscaled = scaled_grad.reshape(TOKENS, BLOCK, groups) / block_scale
    d_tokens = rotate_rows(unscaled).reshape(TOKENS, D).astype(jnp.bfloat16)
    return (mixed, d_tokens, grad_gate, grad_up, grad_down)
```

```python
import math

import jax
import jax.numpy as jnp
from jax import lax
from jax.experimental import pallas as pl
from jax.experimental.pallas import tpu as pltpu
from jax.sharding import PartitionSpec as P

BLOCK = 128
LANES = 128
F32 = jnp.float32
BF16 = jnp.bfloat16


def swap(value, axis, distance):
    count = lax.axis_size(axis)
    return lax.ppermute(value, axis, [(i, i ^ distance) for i in range(count)])


def gather_tensor(value):
    half = value.shape[0] // 2
    parts = []
    for rows, steps in ((value[:half], (1, 4)), (value[half:], (4, 1))):
        for step in steps:
            rows = jnp.concatenate(
                [rows] + [swap(rows, "tensor", step * d) for d in (1, 3, 2)], axis=0
            )
        parts.append(rows)
    return jnp.concatenate(parts, axis=0)


def scatter_tensor(value):
    half = value.shape[0] // 2
    parts = []
    for rows, steps in ((value[:half], (4, 1)), (value[half:], (1, 4))):
        for step in steps:
            size = rows.shape[0] // 4
            total = rows[:size]
            for i, d in enumerate((1, 3, 2)):
                sent = rows[size * (i + 1) : size * (i + 2)].astype(BF16)
                total = total + swap(sent, "tensor", step * d).astype(F32)
            rows = total
        parts.append(rows)
    return jnp.concatenate(parts, axis=0)


OWNERS = (0, 2, 6, 4, 1, 3, 7, 5)


def to_relative(value, me):
    size = value.shape[0] // 8
    return jnp.concatenate(
        [lax.dynamic_slice_in_dim(value, (me ^ p) * size, size) for p in OWNERS], axis=0
    )


def to_absolute(value, me):
    size = value.shape[0] // 8
    place = jnp.array([OWNERS.index(p) for p in range(8)], jnp.int32)
    return jnp.concatenate(
        [lax.dynamic_slice_in_dim(value, place[me ^ o] * size, size) for o in range(8)], axis=0
    )


def gather_dp(value):
    same = jnp.concatenate(
        [value] + [swap(value, "dp", 2 * d) for d in (1, 3, 2)], axis=0
    )
    return jnp.concatenate([same, swap(same, "dp", 1)], axis=0)


def scatter_dp(rows, weight, dims):
    half = rows.shape[0] // 2
    size = half // 4
    other = lax.dot_general(
        rows[half:], weight, (dims, ((), ())), preferred_element_type=F32
    ).astype(BF16)
    other = swap(other, "dp", 1)
    mine = lax.dot_general(rows[:half], weight, (dims, ((), ())), preferred_element_type=F32)
    mine = mine + other.astype(F32)
    total = mine[:size]
    for i, d in enumerate((1, 3, 2)):
        sent = mine[size * (i + 1) : size * (i + 2)].astype(BF16)
        total = total + swap(sent, "dp", 2 * d).astype(F32)
    return total


def butterfly(tiles):
    count = len(tiles)
    distance = 1
    while distance < count:
        done = list(tiles)
        for i in range(count):
            if not i & distance:
                done[i] = tiles[i] + tiles[i | distance]
                done[i | distance] = tiles[i] - tiles[i | distance]
        tiles = done
        distance *= 2
    return tiles


def lane_butterfly(tile):
    lane = lax.broadcasted_iota(jnp.int32, tile.shape, 1)
    turned = pltpu.roll(tile, LANES // 2, 1)
    return jnp.where(lane < LANES // 2, tile + turned, turned - tile)


def block_tiles(refs, distance, groups):
    place = (0, 1, 3, 2).index(distance // 2)
    if distance & 1:
        ref = refs[4]
        rows = pl.ds(pl.multiple_of(pl.program_id(0) * 16 + place * groups, 16), 16)
    else:
        ref = refs[place]
        rows = pl.ds(pl.multiple_of(pl.program_id(0) * 16, 16), 16)
    return [ref[rows, q * LANES : (q + 1) * LANES].astype(F32) for q in range(8)]


def rotate_kernel(me_ref, *refs):
    *parts, scaled_ref, scale_ref, hold = refs
    me = me_ref[0]
    row_count = parts[0].shape[0]
    for d in range(8):
        tiles = [lane_butterfly(t) for t in butterfly(block_tiles(parts, d, row_count))]
        for q in range(8):
            hold[d * 8 + q] = tiles[q]
    largest = None
    for q in range(8):
        tiles = butterfly([hold[d * 8 + q] for d in range(8)])
        for d in range(8):
            hold[d * 8 + q] = tiles[d]
            size = jnp.abs(tiles[d])
            largest = size if largest is None else jnp.maximum(largest, size)
    largest = jnp.maximum(largest, pltpu.roll(largest, LANES // 2, 1))
    scale = largest / math.sqrt(BLOCK) + 1e-05
    parity = (me ^ (me >> 1) ^ (me >> 2)) & 1
    sign = (1 - 2 * parity).astype(F32)
    for q in range(8):
        columns = slice(q * LANES, (q + 1) * LANES)
        rotated = hold[me * 8 + q] * sign / math.sqrt(BLOCK)
        scaled_ref[:, columns] = (rotated / scale).astype(BF16)
        scale_ref[:, columns] = scale


def unrotate_kernel(me_ref, *refs):
    *parts, out_ref = refs
    me = me_ref[0]
    row_count = parts[0].shape[0]
    total = None
    for d in range(8):
        both = (me ^ d) & me
        parity = (both ^ (both >> 1) ^ (both >> 2)) & 1
        sign = (1 - 2 * parity).astype(F32)
        tiles = [t * sign for t in block_tiles(parts, d, row_count)]
        total = tiles if total is None else [a + b for a, b in zip(total, tiles)]
    tiles = [lane_butterfly(t) for t in butterfly(total)]
    for q in range(8):
        out_ref[:, q * LANES : (q + 1) * LANES] = (tiles[q] / math.sqrt(BLOCK)).astype(BF16)


def dp_blocks(value):
    near = [value] + [swap(value, "dp", 2 * d) for d in (1, 3, 2)]
    return near + [swap(jnp.concatenate(near, axis=0), "dp", 1)]


def whole(shape):
    return pl.BlockSpec(shape, lambda i, me: (0, 0))


def rotate(tokens, me):
    rows, width = tokens.shape
    parts = dp_blocks(tokens)
    return pl.pallas_call(
        rotate_kernel,
        grid_spec=pltpu.PrefetchScalarGridSpec(
            num_scalar_prefetch=1,
            grid=(rows // 16,),
            in_specs=[whole(p.shape) for p in parts],
            out_specs=[pl.BlockSpec((16, width), lambda i, me: (i, 0))] * 2,
            scratch_shapes=[pltpu.VMEM((64, 16, LANES), F32)],
        ),
        out_shape=[
            jax.ShapeDtypeStruct((rows, width), BF16),
            jax.ShapeDtypeStruct((rows, width), F32),
        ],
        compiler_params=pltpu.CompilerParams(vmem_limit_bytes=24 * 1024 * 1024),
    )(me[None], *parts)


def unrotate(values, me):
    rows, width = values.shape
    parts = dp_blocks(values)
    return pl.pallas_call(
        unrotate_kernel,
        grid_spec=pltpu.PrefetchScalarGridSpec(
            num_scalar_prefetch=1,
            grid=(rows // 16,),
            in_specs=[whole(p.shape) for p in parts],
            out_specs=pl.BlockSpec((16, width), lambda i, me: (i, 0)),
        ),
        out_shape=jax.ShapeDtypeStruct((rows, width), BF16),
        compiler_params=pltpu.CompilerParams(vmem_limit_bytes=24 * 1024 * 1024),
    )(me[None], *parts)


def local(tokens, gate_weight, up_weight, down_weight, d_mixed):
    me = lax.axis_index("dp").astype(jnp.int32)
    hidden_share = gate_weight.shape[1]
    with jax.named_scope("rotate"):
        scaled, block_scale = rotate(tokens, me)
    with jax.named_scope("gather_cotangent"):
        cotangent = to_relative(gather_tensor(d_mixed), me)
    with jax.named_scope("hidden_grad"):
        hidden_grad = scatter_dp(cotangent, down_weight, ((1,), (1,)))
    weight_pair = jnp.concatenate([gate_weight, up_weight], axis=1)
    with jax.named_scope("gather_scaled"):
        scaled_all = to_relative(gather_tensor(scaled), me)
    with jax.named_scope("gate_up"):
        gate_up = scatter_dp(scaled_all, weight_pair, ((1,), (0,)))
    gate = gate_up[:, :hidden_share]
    up = gate_up[:, hidden_share:]
    sigmoid_gate = jax.nn.sigmoid(gate)
    silu_gate = gate * sigmoid_gate
    hidden = (silu_gate * up).astype(BF16)
    gate_grad = (
        hidden_grad * up * sigmoid_gate * (1.0 + gate * (1.0 - sigmoid_gate))
    ).astype(BF16)
    up_grad = (hidden_grad * silu_gate).astype(BF16)
    with jax.named_scope("gather_hidden"):
        hidden_all = gather_dp(hidden)
    with jax.named_scope("mixed"):
        mixed = scatter_tensor(
            jnp.dot(to_absolute(hidden_all, me), down_weight, preferred_element_type=F32)
        ).astype(BF16)
    with jax.named_scope("gather_grad"):
        grad_pair = gather_dp(jnp.concatenate([gate_grad, up_grad], axis=1))
    with jax.named_scope("scaled_grad"):
        scaled_grad = scatter_tensor(
            lax.dot_general(
                to_absolute(grad_pair, me),
                weight_pair,
                (((1,), (1,)), ((), ())),
                preferred_element_type=F32,
            )
        )
    with jax.named_scope("weight_grads"):
        rows_first = (((0,), (0,)), ((), ()))
        grad_down = lax.dot_general(
            hidden_all, cotangent, rows_first, preferred_element_type=F32
        )
        grad_gate = lax.dot_general(
            scaled_all, grad_pair[:, :hidden_share], rows_first, preferred_element_type=F32
        )
        grad_up = lax.dot_general(
            scaled_all, grad_pair[:, hidden_share:], rows_first, preferred_element_type=F32
        )
    with jax.named_scope("unrotate"):
        d_tokens = unrotate((scaled_grad / block_scale).astype(BF16), me)
    return (mixed, d_tokens, grad_gate, grad_up, grad_down)


def solution(mesh):
    tokens = P("tensor", "dp")
    weight = P("dp", "tensor")
    down = P("tensor", "dp")
    return jax.shard_map(
        local,
        mesh=mesh,
        in_specs=(tokens, weight, weight, down, tokens),
        out_specs=(tokens, tokens, weight, weight, down),
        check_vma=False,
    )
```

```python
import math

import jax
import jax.numpy as jnp
from jax import lax
from jax.experimental import pallas as pl
from jax.experimental.pallas import tpu as pltpu
from jax.sharding import Mesh, PartitionSpec as P

BLOCK = 128
LANES = 128
F32 = jnp.float32
BF16 = jnp.bfloat16


def swap(value, axis, distance):
    count = lax.axis_size(axis)
    return lax.ppermute(value, axis, [(i, i ^ distance) for i in range(count)])


NONE = pl.CostEstimate(flops=0, bytes_accessed=0, transcendentals=0)


def product_kernel(rows_ref, weight_ref, out_ref):
    out_ref[...] = lax.dot_general(
        rows_ref[...], weight_ref[...], (((1,), (1,)), ((), ())), preferred_element_type=F32
    ).astype(out_ref.dtype)


def product(rows, first, count, weight, dtype):
    steps = 2
    size = count // steps
    depth = rows.shape[1]
    return pl.pallas_call(
        product_kernel,
        grid=(steps,),
        in_specs=[
            pl.BlockSpec((size, depth), lambda i: (first * steps + i, 0)),
            pl.BlockSpec(weight.shape, lambda i: (0, 0)),
        ],
        out_specs=pl.BlockSpec((size, weight.shape[0]), lambda i: (i, 0)),
        out_shape=jax.ShapeDtypeStruct((count, weight.shape[0]), dtype),
        cost_estimate=NONE,
        compiler_params=pltpu.CompilerParams(vmem_limit_bytes=32 * 1024 * 1024),
    )(rows, weight)


def place(pieces, moves, positions, rows, out_rows):
    width = max(column + pieces[piece].shape[1] for piece, _, _, column in moves)

    def kernel(position_ref, *refs):
        *ins, out = refs
        for piece, row, where, column in moves:
            target = pl.multiple_of(position_ref[where] * rows, rows)
            block = ins[piece][row : row + rows, :]
            out[pl.ds(target, rows), column : column + block.shape[1]] = block

    return pl.pallas_call(
        kernel,
        grid_spec=pltpu.PrefetchScalarGridSpec(
            num_scalar_prefetch=1,
            grid=(1,),
            in_specs=[whole(piece.shape) for piece in pieces],
            out_specs=whole((out_rows, width)),
        ),
        out_shape=jax.ShapeDtypeStruct((out_rows, width), pieces[0].dtype),
        cost_estimate=NONE,
        compiler_params=pltpu.CompilerParams(vmem_limit_bytes=32 * 1024 * 1024),
    )(positions, *pieces)


def after(value, *earlier):
    return lax.optimization_barrier((value, *earlier))[0]


def swaps(value, axis):
    return [value] + [swap(value, axis, d) for d in ORDER[1:]]


ORDER = (0, 1, 3, 2)


RELAYED = (0, 1, 3, 2, 2)


def relay_start(pieces, axis):
    half = pieces[3].shape[0] // 2
    sent = pieces[3].astype(BF16)
    return swap(sent[:half], axis, 1), swap(sent[half:], axis, 3)


def relay_middle(pieces, received):
    one, three = pieces[1:3]
    half = one.shape[0] // 2
    first, second = [r.astype(F32) for r in received]
    three = jnp.concatenate([three[:half] + first, three[half:]], axis=0).astype(BF16)
    one = jnp.concatenate([one[:half], one[half:] + second], axis=0).astype(BF16)
    return three, one


def relay_end(middle, axis):
    three, one = middle
    return [swap(three, axis, 3), swap(one, axis, 1)]


def gather_place(pieces, first_outer):
    rows = pieces[0].shape[0] // 4
    moves = []
    for i, outer in enumerate(RELAYED):
        for j in range(pieces[i].shape[0] // rows):
            inner = ORDER[j + 2 * (i == 4)]
            y, x = (outer, inner) if first_outer == "y" else (inner, outer)
            moves.append((i, j * rows, y * 4 + x, 0))
    block = (lax.axis_index("y") * 4 + lax.axis_index("x")) ^ jnp.arange(16, dtype=jnp.int32)
    block = (block >> 1 & 1 ^ lax.axis_index("core")) * 8 + (block >> 2) * 2 + (block & 1)
    return place(pieces, moves, block, rows, 16 * rows)


def send(own, pieces, axis):
    return own, [swap(p.astype(BF16), axis, d) for p, d in zip(pieces, ORDER[1:])]


def mixed_pieces(value):
    rows = value.shape[0] // 16
    width = value.shape[1]
    x, core = lax.axis_index("x"), lax.axis_index("core")
    grid = value.reshape(2, 4, 2, rows, width)
    return [
        lax.dynamic_slice(
            grid, ((x ^ d) // 2 ^ core, 0, (x ^ d) % 2, 0, 0), (1, 4, 1, rows, width)
        ).reshape(4 * rows, width)
        for d in ORDER
    ]


def mixed_last(total):
    rows = total.shape[0] // 4
    y = lax.axis_index("y")
    pieces = [lax.dynamic_slice_in_dim(total, (y ^ d) * rows, rows) for d in ORDER]
    return [pieces[0]] + [p.astype(BF16) for p in pieces[1:]]


def scatter_pieces(mine, other):
    size = mine.shape[0] // 4
    y = lax.axis_index("y")
    return [
        jnp.concatenate(
            [lax.dynamic_slice_in_dim(part, (y ^ d) * size, size) for part in (mine, other)],
            axis=0,
        )
        for d in ORDER
    ]


def scatter_last(total):
    rows = total.shape[0] // 4
    x, core = lax.axis_index("x"), lax.axis_index("core")
    pieces = [
        lax.dynamic_slice_in_dim(
            total, (((x ^ d) // 2 ^ core) * 2 + (x ^ d) % 2) * rows, rows
        )
        for d in ORDER
    ]
    return [pieces[0]] + [p.astype(BF16) for p in pieces[1:]]


def summed(part):
    own, received = part
    for piece in received:
        own = own + piece.astype(F32)
    return own


def gather_z(pieces):
    order = lax.axis_index("z") ^ jnp.array(ORDER, jnp.int32)
    if len(pieces) == 4:
        rows = pieces[0].shape[0]
        return place(pieces, [(i, 0, i, 0) for i in range(4)], order, rows, 4 * rows)
    rows = pieces[3].shape[0]
    moves = [(i, j * rows, 2 * i + j, 0) for i in range(3) for j in range(2)]
    moves += [(3, 0, 6, 0), (4, 0, 7, 0)]
    order = 2 * jnp.repeat(order, 2) + jnp.arange(8, dtype=jnp.int32) % 2
    return place(pieces, moves, order, rows, 8 * rows)


def place_cores(mine, other):
    rows = mine.shape[0]
    order = jnp.arange(2, dtype=jnp.int32)
    return place([mine, other], [(0, 0, 0, 0), (1, 0, 1, 0)], order, rows, 2 * rows)


def cores_kernel(order_ref, mine_ref, other_ref, *out_refs):
    total = mine_ref[...] + other_ref[...].astype(F32)
    for i, out_ref in enumerate(out_refs):

        @pl.when(pl.program_id(0) == i)
        def _(out_ref=out_ref):
            out_ref[...] = total.astype(out_ref.dtype)


def core_sums(rows, weight, dims, types, earlier=()):
    z = lax.axis_index("z")
    half = rows.shape[0] // 2
    size = half // 4
    if dims == ((1,), (1,)):
        sent = product(rows, 1, half, weight, BF16)
        other = swap(sent, "core", 1)
        mine = product(after(rows, sent), 0, half, weight, F32)
    else:
        mine, other = rows[:half], rows[half:]
        dims = (dims, ((), ()))
        sent = lax.dot_general(other, weight, dims, preferred_element_type=F32).astype(BF16)
        other = swap(sent, "core", 1)
        mine = lax.dot_general(
            after(mine, sent, *earlier), weight, dims, preferred_element_type=F32
        )
    width = mine.shape[1]
    block = pl.BlockSpec((size, width), lambda i, s: (s[i], 0))
    out = pl.BlockSpec((size, width), lambda i, s: (0, 0))
    one, three, two, own = pl.pallas_call(
        cores_kernel,
        grid_spec=pltpu.PrefetchScalarGridSpec(
            num_scalar_prefetch=1,
            grid=(4,),
            in_specs=[block, block],
            out_specs=[out] * 4,
        ),
        out_shape=[jax.ShapeDtypeStruct((size, width), t) for t in types],
        cost_estimate=NONE,
        compiler_params=pltpu.CompilerParams(vmem_limit_bytes=32 * 1024 * 1024),
    )(z ^ jnp.array((1, 3, 2, 0), jnp.int32), mine, other)
    return [own, one, three, two]


def hidden_kernel(*refs):
    ins, (hidden_ref, pair_ref) = refs[:8], refs[8:]
    share = hidden_ref.shape[1]
    gate, up = [
        summed((ins[0][:, c], [r[:, c] for r in ins[1:4]]))
        for c in (slice(0, share), slice(share, 2 * share))
    ]
    hidden_grad = summed((ins[4][...], [r[...] for r in ins[5:]]))
    sigmoid_gate = jax.nn.sigmoid(gate)
    silu_gate = gate * sigmoid_gate
    hidden_ref[...] = (silu_gate * up).astype(BF16)
    pair_ref[:, :share] = (
        hidden_grad * up * sigmoid_gate * (1.0 + gate * (1.0 - sigmoid_gate))
    ).astype(BF16)
    pair_ref[:, share:] = (hidden_grad * silu_gate).astype(BF16)


def hidden_and_grads(gate_up, hidden_grad):
    ins = [gate_up[0], *gate_up[1], hidden_grad[0], *hidden_grad[1]]
    rows, share = hidden_grad[0].shape
    return pl.pallas_call(
        hidden_kernel,
        grid=(rows // 32,),
        in_specs=[pl.BlockSpec((32, p.shape[1]), lambda i: (i, 0)) for p in ins],
        out_specs=[
            pl.BlockSpec((32, share), lambda i: (i, 0)),
            pl.BlockSpec((32, 2 * share), lambda i: (i, 0)),
        ],
        out_shape=[
            jax.ShapeDtypeStruct((rows, share), BF16),
            jax.ShapeDtypeStruct((rows, 2 * share), BF16),
        ],
        compiler_params=pltpu.CompilerParams(vmem_limit_bytes=32 * 1024 * 1024),
    )(*ins)


def butterfly(tiles):
    count = len(tiles)
    distance = 1
    while distance < count:
        done = list(tiles)
        for i in range(count):
            if not i & distance:
                done[i] = tiles[i] + tiles[i | distance]
                done[i | distance] = tiles[i] - tiles[i | distance]
        tiles = done
        distance *= 2
    return tiles


def lane_butterfly(tile):
    lane = lax.broadcasted_iota(jnp.int32, tile.shape, 1)
    turned = pltpu.roll(tile, LANES // 2, 1)
    return jnp.where(lane < LANES // 2, tile + turned, turned - tile)


def block_tiles(refs, distance, groups):
    place = (0, 1, 3, 2).index(distance // 2)
    if distance & 1:
        ref = refs[4]
        rows = pl.ds(pl.multiple_of(pl.program_id(0) * 16 + place * groups, 16), 16)
    else:
        ref = refs[place]
        rows = pl.ds(pl.multiple_of(pl.program_id(0) * 16, 16), 16)
    return [ref[rows, q * LANES : (q + 1) * LANES].astype(F32) for q in range(8)]


def rotate_kernel(me_ref, *refs):
    *parts, scaled_ref, scale_ref, hold = refs
    me = me_ref[0]
    row_count = parts[0].shape[0]
    for d in range(8):
        tiles = [lane_butterfly(t) for t in butterfly(block_tiles(parts, d, row_count))]
        for q in range(8):
            hold[d * 8 + q] = tiles[q]
    largest = None
    for q in range(8):
        tiles = butterfly([hold[d * 8 + q] for d in range(8)])
        for d in range(8):
            hold[d * 8 + q] = tiles[d]
            size = jnp.abs(tiles[d])
            largest = size if largest is None else jnp.maximum(largest, size)
    largest = jnp.maximum(largest, pltpu.roll(largest, LANES // 2, 1))
    scale = largest / math.sqrt(BLOCK) + 1e-05
    parity = (me ^ (me >> 1) ^ (me >> 2)) & 1
    sign = (1 - 2 * parity).astype(F32)
    for q in range(8):
        columns = slice(q * LANES, (q + 1) * LANES)
        rotated = hold[me * 8 + q] * sign / math.sqrt(BLOCK)
        scaled_ref[:, columns] = (rotated / scale).astype(BF16)
        scale_ref[:, columns] = scale


def unrotate_kernel(me_ref, *refs):
    *parts, out_ref = refs
    me = me_ref[0]
    row_count = parts[0].shape[0]
    total = None
    for d in range(8):
        both = (me ^ d) & me
        parity = (both ^ (both >> 1) ^ (both >> 2)) & 1
        sign = (1 - 2 * parity).astype(F32)
        tiles = [t * sign for t in block_tiles(parts, d, row_count)]
        total = tiles if total is None else [a + b for a, b in zip(total, tiles)]
    tiles = [lane_butterfly(t) for t in butterfly(total)]
    for q in range(8):
        out_ref[:, q * LANES : (q + 1) * LANES] = (tiles[q] / math.sqrt(BLOCK)).astype(BF16)


def dp_blocks(near):
    return near + [swap(jnp.concatenate(near, axis=0), "core", 1)]


def whole(shape):
    return pl.BlockSpec(shape, lambda i, me: (0, 0))


def rotate(parts, me):
    rows, width = parts[0].shape
    return pl.pallas_call(
        rotate_kernel,
        grid_spec=pltpu.PrefetchScalarGridSpec(
            num_scalar_prefetch=1,
            grid=(rows // 16,),
            in_specs=[whole(p.shape) for p in parts],
            out_specs=[pl.BlockSpec((16, width), lambda i, me: (i, 0))] * 2,
            scratch_shapes=[pltpu.VMEM((64, 16, LANES), F32)],
        ),
        out_shape=[
            jax.ShapeDtypeStruct((rows, width), BF16),
            jax.ShapeDtypeStruct((rows, width), F32),
        ],
        compiler_params=pltpu.CompilerParams(vmem_limit_bytes=24 * 1024 * 1024),
    )(me[None], *parts)


def unrotate(parts, me):
    rows, width = parts[0].shape
    return pl.pallas_call(
        unrotate_kernel,
        grid_spec=pltpu.PrefetchScalarGridSpec(
            num_scalar_prefetch=1,
            grid=(rows // 16,),
            in_specs=[whole(p.shape) for p in parts],
            out_specs=pl.BlockSpec((16, width), lambda i, me: (i, 0)),
        ),
        out_shape=jax.ShapeDtypeStruct((rows, width), BF16),
        compiler_params=pltpu.CompilerParams(vmem_limit_bytes=24 * 1024 * 1024),
    )(me[None], *parts)


def local(tokens, gate_weight, up_weight, down_weight, d_mixed):
    me = lax.axis_index("z") * 2 + lax.axis_index("core")
    hidden_share = gate_weight.shape[1]
    rows_first = (((0,), (0,)), ((), ()))
    weight_pair = jnp.concatenate([gate_weight, up_weight], axis=1)

    scaled, block_scale = rotate(dp_blocks(swaps(tokens, "z")), me)
    scaled = jnp.concatenate(swaps(scaled, "x"), axis=0)
    cot = jnp.concatenate(swaps(d_mixed, "y"), axis=0)
    scaled, cot = lax.optimization_barrier((scaled, cot))
    half = cot.shape[0] // 2
    one, three = swap(scaled, "y", 1), swap(scaled, "y", 3)
    cot_one, cot_three = swap(cot, "x", 1), swap(cot, "x", 3)
    first, second = three[:half], one[half:]
    scaled = [scaled, one, three, swap(first, "y", 1), swap(second, "y", 3)]
    cot_first = after(cot_three[:half], first, second)
    cot_second = after(cot_one[half:], first, second)
    cot = [cot, cot_one, cot_three, swap(cot_first, "x", 1), swap(cot_second, "x", 3)]

    scaled[0] = after(scaled[0], cot_first, cot_second)
    scaled_all = gather_place(scaled, "y")
    types = (BF16, BF16, BF16, F32)
    gate_up = core_sums(scaled_all, weight_pair, ((1,), (0,)), types)
    cot[0] = after(cot[0], gate_up[0])
    cot = gather_place(cot, "x")
    gate_up = send(gate_up[0], gate_up[1:], "z")
    hidden_grad = core_sums(cot, down_weight, ((1,), (1,)), types)
    hidden_grad = send(hidden_grad[0], hidden_grad[1:], "z")
    hidden, grad_pair = hidden_and_grads(gate_up, hidden_grad)

    hidden_pieces = swaps(hidden, "z")
    grad_pair = after(grad_pair, *hidden_pieces[1:])
    grad_one, grad_three = swap(grad_pair, "z", 1), swap(grad_pair, "z", 3)
    hidden_mine = gather_z(hidden_pieces)
    hidden_all = place_cores(hidden_mine, swap(hidden_mine, "core", 1))
    mixed = mixed_pieces(jnp.dot(hidden_all, down_weight, preferred_element_type=F32))
    mixed_received = relay_start(mixed, "x")
    half = grad_pair.shape[0] // 2
    first, second = after(grad_three[:half], mixed[3]), after(grad_one[half:], mixed[3])
    grad_pieces = [grad_pair, grad_one, grad_three, swap(first, "z", 1), swap(second, "z", 3)]
    mixed_received = [after(r, first, second) for r in mixed_received]
    mixed_middle = relay_middle(mixed, mixed_received)
    mixed_received = relay_end(mixed_middle, "x")
    grad_down = lax.dot_general(
        after(hidden_all, *mixed_middle), cot, rows_first, preferred_element_type=F32
    )

    grad_mine = gather_z([after(grad_pair, grad_down)] + grad_pieces[1:])
    grad_other = swap(grad_mine, "core", 1)
    dims = (((1,), (1,)), ((), ()))
    partial = lax.dot_general(grad_mine, weight_pair, dims, preferred_element_type=F32)
    partial_other = lax.dot_general(
        after(grad_other, partial), weight_pair, dims, preferred_element_type=F32
    )
    pieces = scatter_pieces(partial, partial_other)
    received = relay_start(pieces, "y")
    mixed = mixed_last(summed((after(mixed[0], pieces[3]), mixed_received)))
    mixed_received = send(mixed[0], mixed[1:], "y")[1]
    grad_all = place_cores(after(grad_mine, *mixed[1:]), grad_other)
    received = [after(r, grad_all) for r in received]
    middle = relay_middle(pieces, received)
    received = relay_end(middle, "y")
    grad_gate = lax.dot_general(
        after(scaled_all, *middle),
        grad_all[:, :hidden_share],
        rows_first,
        preferred_element_type=F32,
    )
    grad_up = lax.dot_general(
        after(scaled_all, *middle),
        grad_all[:, hidden_share:],
        rows_first,
        preferred_element_type=F32,
    )
    last = scatter_last(summed((after(pieces[0], grad_gate, grad_up), received)))
    received = send(last[0], last[1:], "x")[1]
    mixed = summed((after(mixed[0], *last[1:]), mixed_received)).astype(BF16)
    scaled_grad = summed((after(last[0], mixed), received))
    d_tokens = unrotate(dp_blocks(swaps((scaled_grad / block_scale).astype(BF16), "z")), me)
    return (mixed, d_tokens, grad_gate, grad_up, grad_down)


def solution(mesh):
    split = Mesh(mesh.devices.reshape(4, 2, 4, 4), ("z", "core", "y", "x"))
    tokens = P(("y", "x"), ("z", "core"))
    weight = P(("z", "core"), ("y", "x"))
    down = P(("y", "x"), ("z", "core"))
    return jax.shard_map(
        local,
        mesh=split,
        in_specs=(tokens, weight, weight, down, tokens),
        out_specs=(tokens, tokens, weight, weight, down),
        check_vma=False,
    )
```

```python
import math

import jax
import jax.numpy as jnp
from jax import lax
from jax.experimental import pallas as pl
from jax.experimental.pallas import tpu as pltpu
from jax.sharding import Mesh, PartitionSpec as P

BLOCK = 128
LANES = 128
F32 = jnp.float32
BF16 = jnp.bfloat16


def swap(value, axis, distance):
    count = lax.axis_size(axis)
    return lax.ppermute(value, axis, [(i, i ^ distance) for i in range(count)])


NONE = pl.CostEstimate(flops=0, bytes_accessed=0, transcendentals=0)


def product_kernel(rows_ref, weight_ref, out_ref):
    out_ref[...] = lax.dot_general(
        rows_ref[...], weight_ref[...], (((1,), (1,)), ((), ())), preferred_element_type=F32
    ).astype(out_ref.dtype)


def product(rows, first, count, weight, dtype):
    steps = 2
    size = count // steps
    depth = rows.shape[1]
    return pl.pallas_call(
        product_kernel,
        grid=(steps,),
        in_specs=[
            pl.BlockSpec((size, depth), lambda i: (first * steps + i, 0)),
            pl.BlockSpec(weight.shape, lambda i: (0, 0)),
        ],
        out_specs=pl.BlockSpec((size, weight.shape[0]), lambda i: (i, 0)),
        out_shape=jax.ShapeDtypeStruct((count, weight.shape[0]), dtype),
        cost_estimate=NONE,
        compiler_params=pltpu.CompilerParams(vmem_limit_bytes=32 * 1024 * 1024),
    )(rows, weight)


def place(pieces, moves, positions, rows, out_rows):
    width = max(column + pieces[piece].shape[1] for piece, _, _, column in moves)

    def kernel(position_ref, *refs):
        *ins, out = refs
        for piece, row, where, column in moves:
            target = pl.multiple_of(position_ref[where] * rows, rows)
            block = ins[piece][row : row + rows, :]
            out[pl.ds(target, rows), column : column + block.shape[1]] = block

    return pl.pallas_call(
        kernel,
        grid_spec=pltpu.PrefetchScalarGridSpec(
            num_scalar_prefetch=1,
            grid=(1,),
            in_specs=[whole(piece.shape) for piece in pieces],
            out_specs=whole((out_rows, width)),
        ),
        out_shape=jax.ShapeDtypeStruct((out_rows, width), pieces[0].dtype),
        cost_estimate=NONE,
        compiler_params=pltpu.CompilerParams(vmem_limit_bytes=32 * 1024 * 1024),
    )(positions, *pieces)


def after(value, *earlier):
    return lax.optimization_barrier((value, *earlier))[0]


def swaps(value, axis):
    return [value] + [swap(value, axis, d) for d in ORDER[1:]]


ORDER = (0, 1, 3, 2)


RELAYED = (0, 1, 3, 2, 2)


def relay_start(pieces, axis):
    half = pieces[3].shape[0] // 2
    sent = pieces[3].astype(BF16)
    return swap(sent[:half], axis, 1), swap(sent[half:], axis, 3)


def relay_middle(pieces, received):
    one, three = pieces[1:3]
    half = one.shape[0] // 2
    first, second = [r.astype(F32) for r in received]
    three = jnp.concatenate([three[:half] + first, three[half:]], axis=0).astype(BF16)
    one = jnp.concatenate([one[:half], one[half:] + second], axis=0).astype(BF16)
    return three, one


def relay_end(middle, axis):
    three, one = middle
    return [swap(three, axis, 3), swap(one, axis, 1)]


def gather_place(pieces, first_outer):
    rows = pieces[0].shape[0] // 4
    moves = []
    for i, outer in enumerate(RELAYED):
        for j in range(pieces[i].shape[0] // rows):
            inner = ORDER[j + 2 * (i == 4)]
            y, x = (outer, inner) if first_outer == "y" else (inner, outer)
            moves.append((i, j * rows, y * 4 + x, 0))
    block = (lax.axis_index("y") * 4 + lax.axis_index("x")) ^ jnp.arange(16, dtype=jnp.int32)
    block = (block >> 1 & 1 ^ lax.axis_index("core")) * 8 + (block >> 2) * 2 + (block & 1)
    return place(pieces, moves, block, rows, 16 * rows)


def send(own, pieces, axis):
    return own, [swap(p.astype(BF16), axis, d) for p, d in zip(pieces, ORDER[1:])]


def mixed_pieces(value):
    rows = value.shape[0] // 16
    width = value.shape[1]
    x, core = lax.axis_index("x"), lax.axis_index("core")
    grid = value.reshape(2, 4, 2, rows, width)
    return [
        lax.dynamic_slice(
            grid, ((x ^ d) // 2 ^ core, 0, (x ^ d) % 2, 0, 0), (1, 4, 1, rows, width)
        ).reshape(4 * rows, width)
        for d in ORDER
    ]


def mixed_last(total):
    rows = total.shape[0] // 4
    y = lax.axis_index("y")
    pieces = [lax.dynamic_slice_in_dim(total, (y ^ d) * rows, rows) for d in ORDER]
    return [pieces[0]] + [p.astype(BF16) for p in pieces[1:]]


def scatter_pieces(mine, other):
    size = mine.shape[0] // 4
    y = lax.axis_index("y")
    return [
        jnp.concatenate(
            [lax.dynamic_slice_in_dim(part, (y ^ d) * size, size) for part in (mine, other)],
            axis=0,
        )
        for d in ORDER
    ]


def scatter_last(total):
    rows = total.shape[0] // 4
    x, core = lax.axis_index("x"), lax.axis_index("core")
    pieces = [
        lax.dynamic_slice_in_dim(
            total, (((x ^ d) // 2 ^ core) * 2 + (x ^ d) % 2) * rows, rows
        )
        for d in ORDER
    ]
    return [pieces[0]] + [p.astype(BF16) for p in pieces[1:]]


def summed(part):
    own, received = part
    for piece in received:
        own = own + piece.astype(F32)
    return own


def gather_z(pieces):
    order = lax.axis_index("z") ^ jnp.array(ORDER, jnp.int32)
    if len(pieces) == 4:
        rows = pieces[0].shape[0]
        return place(pieces, [(i, 0, i, 0) for i in range(4)], order, rows, 4 * rows)
    rows = pieces[3].shape[0]
    moves = [(i, j * rows, 2 * i + j, 0) for i in range(3) for j in range(2)]
    moves += [(3, 0, 6, 0), (4, 0, 7, 0)]
    order = 2 * jnp.repeat(order, 2) + jnp.arange(8, dtype=jnp.int32) % 2
    return place(pieces, moves, order, rows, 8 * rows)


def place_cores(mine, other):
    rows = mine.shape[0]
    order = jnp.arange(2, dtype=jnp.int32)
    return place([mine, other], [(0, 0, 0, 0), (1, 0, 1, 0)], order, rows, 2 * rows)


def cores_kernel(order_ref, mine_ref, other_ref, *out_refs):
    total = mine_ref[...] + other_ref[...].astype(F32)
    for i, out_ref in enumerate(out_refs):

        @pl.when(pl.program_id(0) == i)
        def _(out_ref=out_ref):
            out_ref[...] = total.astype(out_ref.dtype)


def core_sums(rows, weight, dims, types, earlier=()):
    z = lax.axis_index("z")
    half = rows.shape[0] // 2
    size = half // 4
    if dims == ((1,), (1,)):
        sent = product(rows, 1, half, weight, BF16)
        other = swap(sent, "core", 1)
        mine = product(after(rows, sent), 0, half, weight, F32)
    else:
        mine, other = rows[:half], rows[half:]
        dims = (dims, ((), ()))
        sent = lax.dot_general(other, weight, dims, preferred_element_type=F32).astype(BF16)
        other = swap(sent, "core", 1)
        mine = lax.dot_general(
            after(mine, sent, *earlier), weight, dims, preferred_element_type=F32
        )
    width = mine.shape[1]
    block = pl.BlockSpec((size, width), lambda i, s: (s[i], 0))
    out = pl.BlockSpec((size, width), lambda i, s: (0, 0))
    one, three, two, own = pl.pallas_call(
        cores_kernel,
        grid_spec=pltpu.PrefetchScalarGridSpec(
            num_scalar_prefetch=1,
            grid=(4,),
            in_specs=[block, block],
            out_specs=[out] * 4,
        ),
        out_shape=[jax.ShapeDtypeStruct((size, width), t) for t in types],
        cost_estimate=NONE,
        compiler_params=pltpu.CompilerParams(vmem_limit_bytes=32 * 1024 * 1024),
    )(z ^ jnp.array((1, 3, 2, 0), jnp.int32), mine, other)
    return [own, one, three, two]


def hidden_kernel(*refs):
    ins, (hidden_ref, pair_ref) = refs[:8], refs[8:]
    share = hidden_ref.shape[1]
    gate, up = [
        summed((ins[0][:, c], [r[:, c] for r in ins[1:4]]))
        for c in (slice(0, share), slice(share, 2 * share))
    ]
    hidden_grad = summed((ins[4][...], [r[...] for r in ins[5:]]))
    sigmoid_gate = jax.nn.sigmoid(gate)
    silu_gate = gate * sigmoid_gate
    hidden_ref[...] = (silu_gate * up).astype(BF16)
    pair_ref[:, :share] = (
        hidden_grad * up * sigmoid_gate * (1.0 + gate * (1.0 - sigmoid_gate))
    ).astype(BF16)
    pair_ref[:, share:] = (hidden_grad * silu_gate).astype(BF16)


def hidden_and_grads(gate_up, hidden_grad):
    ins = [gate_up[0], *gate_up[1], hidden_grad[0], *hidden_grad[1]]
    rows, share = hidden_grad[0].shape
    return pl.pallas_call(
        hidden_kernel,
        grid=(rows // 32,),
        in_specs=[pl.BlockSpec((32, p.shape[1]), lambda i: (i, 0)) for p in ins],
        out_specs=[
            pl.BlockSpec((32, share), lambda i: (i, 0)),
            pl.BlockSpec((32, 2 * share), lambda i: (i, 0)),
        ],
        out_shape=[
            jax.ShapeDtypeStruct((rows, share), BF16),
            jax.ShapeDtypeStruct((rows, 2 * share), BF16),
        ],
        compiler_params=pltpu.CompilerParams(vmem_limit_bytes=32 * 1024 * 1024),
    )(*ins)


def butterfly(tiles):
    count = len(tiles)
    distance = 1
    while distance < count:
        done = list(tiles)
        for i in range(count):
            if not i & distance:
                done[i] = tiles[i] + tiles[i | distance]
                done[i | distance] = tiles[i] - tiles[i | distance]
        tiles = done
        distance *= 2
    return tiles


def lane_butterfly(tile):
    lane = lax.broadcasted_iota(jnp.int32, tile.shape, 1)
    turned = pltpu.roll(tile, LANES // 2, 1)
    return jnp.where(lane < LANES // 2, tile + turned, turned - tile)


def block_tiles(refs, distance, groups):
    place = (0, 1, 3, 2).index(distance // 2)
    if distance & 1:
        ref = refs[4]
        rows = pl.ds(pl.multiple_of(pl.program_id(0) * 16 + place * groups, 16), 16)
    else:
        ref = refs[place]
        rows = pl.ds(pl.multiple_of(pl.program_id(0) * 16, 16), 16)
    return [ref[rows, q * LANES : (q + 1) * LANES].astype(F32) for q in range(8)]


def rotate_kernel(me_ref, *refs):
    *parts, scaled_ref, scale_ref, hold = refs
    me = me_ref[0]
    row_count = parts[0].shape[0]
    for d in range(8):
        tiles = [lane_butterfly(t) for t in butterfly(block_tiles(parts, d, row_count))]
        for q in range(8):
            hold[d * 8 + q] = tiles[q]
    largest = None
    for q in range(8):
        tiles = butterfly([hold[d * 8 + q] for d in range(8)])
        for d in range(8):
            hold[d * 8 + q] = tiles[d]
            size = jnp.abs(tiles[d])
            largest = size if largest is None else jnp.maximum(largest, size)
    largest = jnp.maximum(largest, pltpu.roll(largest, LANES // 2, 1))
    scale = largest / math.sqrt(BLOCK) + 1e-05
    parity = (me ^ (me >> 1) ^ (me >> 2)) & 1
    sign = (1 - 2 * parity).astype(F32)
    for q in range(8):
        columns = slice(q * LANES, (q + 1) * LANES)
        rotated = hold[me * 8 + q] * sign / math.sqrt(BLOCK)
        scaled_ref[:, columns] = (rotated / scale).astype(BF16)
        scale_ref[:, columns] = scale


def unrotate_kernel(me_ref, *refs):
    *parts, out_ref = refs
    me = me_ref[0]
    row_count = parts[0].shape[0]
    total = None
    for d in range(8):
        both = (me ^ d) & me
        parity = (both ^ (both >> 1) ^ (both >> 2)) & 1
        sign = (1 - 2 * parity).astype(F32)
        tiles = [t * sign for t in block_tiles(parts, d, row_count)]
        total = tiles if total is None else [a + b for a, b in zip(total, tiles)]
    tiles = [lane_butterfly(t) for t in butterfly(total)]
    for q in range(8):
        out_ref[:, q * LANES : (q + 1) * LANES] = (tiles[q] / math.sqrt(BLOCK)).astype(BF16)


def dp_blocks(near):
    return near + [swap(jnp.concatenate(near, axis=0), "core", 1)]


def whole(shape):
    return pl.BlockSpec(shape, lambda i, me: (0, 0))


def rotate(parts, me):
    rows, width = parts[0].shape
    return pl.pallas_call(
        rotate_kernel,
        grid_spec=pltpu.PrefetchScalarGridSpec(
            num_scalar_prefetch=1,
            grid=(rows // 16,),
            in_specs=[whole(p.shape) for p in parts],
            out_specs=[pl.BlockSpec((16, width), lambda i, me: (i, 0))] * 2,
            scratch_shapes=[pltpu.VMEM((64, 16, LANES), F32)],
        ),
        out_shape=[
            jax.ShapeDtypeStruct((rows, width), BF16),
            jax.ShapeDtypeStruct((rows, width), F32),
        ],
        compiler_params=pltpu.CompilerParams(vmem_limit_bytes=24 * 1024 * 1024),
    )(me[None], *parts)


def unrotate(parts, me):
    rows, width = parts[0].shape
    return pl.pallas_call(
        unrotate_kernel,
        grid_spec=pltpu.PrefetchScalarGridSpec(
            num_scalar_prefetch=1,
            grid=(rows // 16,),
            in_specs=[whole(p.shape) for p in parts],
            out_specs=pl.BlockSpec((16, width), lambda i, me: (i, 0)),
        ),
        out_shape=jax.ShapeDtypeStruct((rows, width), BF16),
        compiler_params=pltpu.CompilerParams(vmem_limit_bytes=24 * 1024 * 1024),
    )(me[None], *parts)


def local(tokens, gate_weight, up_weight, down_weight, d_mixed):
    me = lax.axis_index("z") * 2 + lax.axis_index("core")
    hidden_share = gate_weight.shape[1]
    rows_first = (((0,), (0,)), ((), ()))
    weight_pair = jnp.concatenate([gate_weight, up_weight], axis=1)

    scaled, block_scale = rotate(dp_blocks(swaps(tokens, "z")), me)
    scaled = jnp.concatenate(swaps(scaled, "x"), axis=0)
    cot = jnp.concatenate(swaps(d_mixed, "y"), axis=0)
    scaled, cot = lax.optimization_barrier((scaled, cot))
    half = cot.shape[0] // 2
    one, three = swap(scaled, "y", 1), swap(scaled, "y", 3)
    cot_one, cot_three = swap(cot, "x", 1), swap(cot, "x", 3)
    first, second = three[:half], one[half:]
    scaled = [scaled, one, three, swap(first, "y", 1), swap(second, "y", 3)]
    cot_first = after(cot_three[:half], first, second)
    cot_second = after(cot_one[half:], first, second)
    cot = [cot, cot_one, cot_three, swap(cot_first, "x", 1), swap(cot_second, "x", 3)]

    scaled[0] = after(scaled[0], cot_first, cot_second)
    scaled_all = gather_place(scaled, "y")
    types = (BF16, BF16, BF16, F32)
    gate_up = core_sums(scaled_all, weight_pair, ((1,), (0,)), types)
    cot[0] = after(cot[0], gate_up[0])
    cot = gather_place(cot, "x")
    gate_up = send(gate_up[0], gate_up[1:], "z")
    hidden_grad = core_sums(cot, down_weight, ((1,), (1,)), types)
    hidden_grad = send(hidden_grad[0], hidden_grad[1:], "z")
    hidden, grad_pair = hidden_and_grads(gate_up, hidden_grad)

    hidden_pieces = swaps(hidden, "z")
    grad_pair = after(grad_pair, *hidden_pieces[1:])
    grad_one, grad_three = swap(grad_pair, "z", 1), swap(grad_pair, "z", 3)
    hidden_mine = gather_z(hidden_pieces)
    hidden_all = place_cores(hidden_mine, swap(hidden_mine, "core", 1))
    mixed = mixed_pieces(jnp.dot(hidden_all, down_weight, preferred_element_type=F32))
    mixed_received = relay_start(mixed, "x")
    half = grad_pair.shape[0] // 2
    first, second = after(grad_three[:half], mixed[3]), after(grad_one[half:], mixed[3])
    grad_pieces = [grad_pair, grad_one, grad_three, swap(first, "z", 1), swap(second, "z", 3)]
    mixed_received = [after(r, first, second) for r in mixed_received]
    mixed_middle = relay_middle(mixed, mixed_received)
    mixed_received = relay_end(mixed_middle, "x")
    grad_mine = gather_z([after(grad_pair, *mixed_middle)] + grad_pieces[1:])
    grad_other = swap(grad_mine, "core", 1)
    dims = (((1,), (1,)), ((), ()))
    partial = lax.dot_general(grad_mine, weight_pair, dims, preferred_element_type=F32)
    partial_other = lax.dot_general(
        after(grad_other, partial), weight_pair, dims, preferred_element_type=F32
    )
    pieces = scatter_pieces(partial, partial_other)
    received = relay_start(pieces, "y")
    middle = relay_middle(pieces, received)
    received = relay_end(middle, "y")
    mixed = mixed_last(summed((after(mixed[0], *middle), mixed_received)))
    mixed_received = send(mixed[0], mixed[1:], "y")[1]
    grad_all = place_cores(after(grad_mine, *mixed[1:]), grad_other)
    grad_gate = lax.dot_general(
        scaled_all, grad_all[:, :hidden_share], rows_first, preferred_element_type=F32
    )
    own = after(pieces[0], grad_gate, *mixed_received)
    last = scatter_last(summed((own, received)))
    received = send(last[0], last[1:], "x")[1]
    grad_up = lax.dot_general(
        after(scaled_all, *last[1:]),
        grad_all[:, hidden_share:],
        rows_first,
        preferred_element_type=F32,
    )
    scaled_grad = summed((after(last[0], grad_up), received))
    unscaled = (scaled_grad / block_scale).astype(BF16)
    near = swaps(unscaled, "z")
    mixed = summed((after(mixed[0], unscaled), mixed_received)).astype(BF16)
    grad_down = lax.dot_general(
        after(hidden_all, unscaled), cot, rows_first, preferred_element_type=F32
    )
    d_tokens = unrotate(dp_blocks([after(near[0], grad_down)] + near[1:]), me)
    return (mixed, d_tokens, grad_gate, grad_up, grad_down)


def solution(mesh):
    split = Mesh(mesh.devices.reshape(4, 2, 4, 4), ("z", "core", "y", "x"))
    tokens = P(("y", "x"), ("z", "core"))
    weight = P(("z", "core"), ("y", "x"))
    down = P(("y", "x"), ("z", "core"))
    return jax.shard_map(
        local,
        mesh=split,
        in_specs=(tokens, weight, weight, down, tokens),
        out_specs=(tokens, tokens, weight, weight, down),
        check_vma=False,
    )
```

```python
import math

import jax
import jax.numpy as jnp
from jax import lax
from jax.experimental import pallas as pl
from jax.experimental.pallas import tpu as pltpu
from jax.sharding import Mesh, PartitionSpec as P

BLOCK = 128
LANES = 128
F32 = jnp.float32
BF16 = jnp.bfloat16


def swap(value, axis, distance):
    count = lax.axis_size(axis)
    return lax.ppermute(value, axis, [(i, i ^ distance) for i in range(count)])


NONE = pl.CostEstimate(flops=0, bytes_accessed=0, transcendentals=0)


def product_kernel(rows_ref, weight_ref, out_ref):
    out_ref[...] = lax.dot_general(
        rows_ref[...], weight_ref[...], (((1,), (1,)), ((), ())), preferred_element_type=F32
    ).astype(out_ref.dtype)


def product(rows, first, count, weight, dtype):
    steps = 2
    size = count // steps
    depth = rows.shape[1]
    return pl.pallas_call(
        product_kernel,
        grid=(steps,),
        in_specs=[
            pl.BlockSpec((size, depth), lambda i: (first * steps + i, 0)),
            pl.BlockSpec(weight.shape, lambda i: (0, 0)),
        ],
        out_specs=pl.BlockSpec((size, weight.shape[0]), lambda i: (i, 0)),
        out_shape=jax.ShapeDtypeStruct((count, weight.shape[0]), dtype),
        cost_estimate=NONE,
        compiler_params=pltpu.CompilerParams(vmem_limit_bytes=32 * 1024 * 1024),
    )(rows, weight)


def place(pieces, moves, positions, rows, out_rows):
    width = max(column + pieces[piece].shape[1] for piece, _, _, column in moves)

    def kernel(position_ref, *refs):
        *ins, out = refs
        for piece, row, where, column in moves:
            target = pl.multiple_of(position_ref[where] * rows, rows)
            block = ins[piece][row : row + rows, :]
            out[pl.ds(target, rows), column : column + block.shape[1]] = block

    return pl.pallas_call(
        kernel,
        grid_spec=pltpu.PrefetchScalarGridSpec(
            num_scalar_prefetch=1,
            grid=(1,),
            in_specs=[whole(piece.shape) for piece in pieces],
            out_specs=whole((out_rows, width)),
        ),
        out_shape=jax.ShapeDtypeStruct((out_rows, width), pieces[0].dtype),
        cost_estimate=NONE,
        compiler_params=pltpu.CompilerParams(vmem_limit_bytes=32 * 1024 * 1024),
    )(positions, *pieces)


def after(value, *earlier):
    return lax.optimization_barrier((value, *earlier))[0]


def swaps(value, axis):
    return [value] + [swap(value, axis, d) for d in ORDER[1:]]


ORDER = (0, 1, 3, 2)


RELAYED = (0, 1, 3, 2, 2)


def relay_start(pieces, axis):
    half = pieces[3].shape[0] // 2
    sent = pieces[3].astype(BF16)
    return swap(sent[:half], axis, 1), swap(sent[half:], axis, 3)


def relay_middle(pieces, received):
    one, three = pieces[1:3]
    half = one.shape[0] // 2
    first, second = [r.astype(F32) for r in received]
    three = jnp.concatenate([three[:half] + first, three[half:]], axis=0).astype(BF16)
    one = jnp.concatenate([one[:half], one[half:] + second], axis=0).astype(BF16)
    return three, one


def relay_end(middle, axis):
    three, one = middle
    return [swap(three, axis, 3), swap(one, axis, 1)]


def gather_place(pieces, first_outer):
    rows = pieces[0].shape[0] // 4
    moves = []
    for i, outer in enumerate(RELAYED):
        for j in range(pieces[i].shape[0] // rows):
            inner = ORDER[j + 2 * (i == 4)]
            y, x = (outer, inner) if first_outer == "y" else (inner, outer)
            moves.append((i, j * rows, y * 4 + x, 0))
    block = (lax.axis_index("y") * 4 + lax.axis_index("x")) ^ jnp.arange(16, dtype=jnp.int32)
    block = (block >> 1 & 1 ^ lax.axis_index("core")) * 8 + (block >> 2) * 2 + (block & 1)
    return place(pieces, moves, block, rows, 16 * rows)


def send(own, pieces, axis):
    return own, [swap(p.astype(BF16), axis, d) for p, d in zip(pieces, ORDER[1:])]


def mixed_pieces(value):
    rows = value.shape[0] // 16
    width = value.shape[1]
    x, core = lax.axis_index("x"), lax.axis_index("core")
    grid = value.reshape(2, 4, 2, rows, width)
    return [
        lax.dynamic_slice(
            grid, ((x ^ d) // 2 ^ core, 0, (x ^ d) % 2, 0, 0), (1, 4, 1, rows, width)
        ).reshape(4 * rows, width)
        for d in ORDER
    ]


def mixed_last(total):
    rows = total.shape[0] // 4
    y = lax.axis_index("y")
    pieces = [lax.dynamic_slice_in_dim(total, (y ^ d) * rows, rows) for d in ORDER]
    return [pieces[0]] + [p.astype(BF16) for p in pieces[1:]]


def scatter_pieces(mine, other):
    size = mine.shape[0] // 4
    y = lax.axis_index("y")
    return [
        jnp.concatenate(
            [lax.dynamic_slice_in_dim(part, (y ^ d) * size, size) for part in (mine, other)],
            axis=0,
        )
        for d in ORDER
    ]


def scatter_last(total):
    rows = total.shape[0] // 4
    x, core = lax.axis_index("x"), lax.axis_index("core")
    pieces = [
        lax.dynamic_slice_in_dim(
            total, (((x ^ d) // 2 ^ core) * 2 + (x ^ d) % 2) * rows, rows
        )
        for d in ORDER
    ]
    return [pieces[0]] + [p.astype(BF16) for p in pieces[1:]]


def summed(part):
    own, received = part
    for piece in received:
        own = own + piece.astype(F32)
    return own


def gather_z(pieces):
    order = lax.axis_index("z") ^ jnp.array(ORDER, jnp.int32)
    if len(pieces) == 4:
        rows = pieces[0].shape[0]
        return place(pieces, [(i, 0, i, 0) for i in range(4)], order, rows, 4 * rows)
    rows = pieces[3].shape[0]
    moves = [(i, j * rows, 2 * i + j, 0) for i in range(3) for j in range(2)]
    moves += [(3, 0, 6, 0), (4, 0, 7, 0)]
    order = 2 * jnp.repeat(order, 2) + jnp.arange(8, dtype=jnp.int32) % 2
    return place(pieces, moves, order, rows, 8 * rows)


def place_cores(mine, other):
    rows = mine.shape[0]
    order = jnp.arange(2, dtype=jnp.int32)
    return place([mine, other], [(0, 0, 0, 0), (1, 0, 1, 0)], order, rows, 2 * rows)


def cores_kernel(order_ref, mine_ref, other_ref, *out_refs):
    total = mine_ref[...] + other_ref[...].astype(F32)
    for i, out_ref in enumerate(out_refs):

        @pl.when(pl.program_id(0) == i)
        def _(out_ref=out_ref):
            out_ref[...] = total.astype(out_ref.dtype)


def core_sums(rows, weight, dims, types, earlier=()):
    z = lax.axis_index("z")
    half = rows.shape[0] // 2
    size = half // 4
    if dims == ((1,), (1,)):
        sent = product(rows, 1, half, weight, BF16)
        other = swap(sent, "core", 1)
        mine = product(after(rows, sent), 0, half, weight, F32)
    else:
        mine, other = rows[:half], rows[half:]
        dims = (dims, ((), ()))
        sent = lax.dot_general(other, weight, dims, preferred_element_type=F32).astype(BF16)
        other = swap(sent, "core", 1)
        mine = lax.dot_general(
            after(mine, sent, *earlier), weight, dims, preferred_element_type=F32
        )
    width = mine.shape[1]
    block = pl.BlockSpec((size, width), lambda i, s: (s[i], 0))
    out = pl.BlockSpec((size, width), lambda i, s: (0, 0))
    one, three, two, own = pl.pallas_call(
        cores_kernel,
        grid_spec=pltpu.PrefetchScalarGridSpec(
            num_scalar_prefetch=1,
            grid=(4,),
            in_specs=[block, block],
            out_specs=[out] * 4,
        ),
        out_shape=[jax.ShapeDtypeStruct((size, width), t) for t in types],
        cost_estimate=NONE,
        compiler_params=pltpu.CompilerParams(vmem_limit_bytes=32 * 1024 * 1024),
    )(z ^ jnp.array((1, 3, 2, 0), jnp.int32), mine, other)
    return [own, one, three, two]


def hidden_kernel(*refs):
    ins, (hidden_ref, pair_ref) = refs[:8], refs[8:]
    share = hidden_ref.shape[1]
    gate, up = [
        summed((ins[0][:, c], [r[:, c] for r in ins[1:4]]))
        for c in (slice(0, share), slice(share, 2 * share))
    ]
    hidden_grad = summed((ins[4][...], [r[...] for r in ins[5:]]))
    sigmoid_gate = jax.nn.sigmoid(gate)
    silu_gate = gate * sigmoid_gate
    hidden_ref[...] = (silu_gate * up).astype(BF16)
    pair_ref[:, :share] = (
        hidden_grad * up * sigmoid_gate * (1.0 + gate * (1.0 - sigmoid_gate))
    ).astype(BF16)
    pair_ref[:, share:] = (hidden_grad * silu_gate).astype(BF16)


def hidden_and_grads(gate_up, hidden_grad):
    ins = [gate_up[0], *gate_up[1], hidden_grad[0], *hidden_grad[1]]
    rows, share = hidden_grad[0].shape
    return pl.pallas_call(
        hidden_kernel,
        grid=(rows // 32,),
        in_specs=[pl.BlockSpec((32, p.shape[1]), lambda i: (i, 0)) for p in ins],
        out_specs=[
            pl.BlockSpec((32, share), lambda i: (i, 0)),
            pl.BlockSpec((32, 2 * share), lambda i: (i, 0)),
        ],
        out_shape=[
            jax.ShapeDtypeStruct((rows, share), BF16),
            jax.ShapeDtypeStruct((rows, 2 * share), BF16),
        ],
        compiler_params=pltpu.CompilerParams(vmem_limit_bytes=32 * 1024 * 1024),
    )(*ins)


def butterfly(tiles):
    count = len(tiles)
    distance = 1
    while distance < count:
        done = list(tiles)
        for i in range(count):
            if not i & distance:
                done[i] = tiles[i] + tiles[i | distance]
                done[i | distance] = tiles[i] - tiles[i | distance]
        tiles = done
        distance *= 2
    return tiles


def lane_butterfly(tile):
    lane = lax.broadcasted_iota(jnp.int32, tile.shape, 1)
    turned = pltpu.roll(tile, LANES // 2, 1)
    return jnp.where(lane < LANES // 2, tile + turned, turned - tile)


def block_tiles(refs, distance, groups):
    place = (0, 1, 3, 2).index(distance // 2)
    if distance & 1:
        ref = refs[4]
        rows = pl.ds(pl.multiple_of(pl.program_id(0) * 16 + place * groups, 16), 16)
    else:
        ref = refs[place]
        rows = pl.ds(pl.multiple_of(pl.program_id(0) * 16, 16), 16)
    return [ref[rows, q * LANES : (q + 1) * LANES].astype(F32) for q in range(8)]


def rotate_kernel(me_ref, *refs):
    *parts, scaled_ref, scale_ref, hold = refs
    me = me_ref[0]
    row_count = parts[0].shape[0]
    for d in range(8):
        tiles = [lane_butterfly(t) for t in butterfly(block_tiles(parts, d, row_count))]
        for q in range(8):
            hold[d * 8 + q] = tiles[q]
    largest = None
    for q in range(8):
        tiles = butterfly([hold[d * 8 + q] for d in range(8)])
        for d in range(8):
            hold[d * 8 + q] = tiles[d]
            size = jnp.abs(tiles[d])
            largest = size if largest is None else jnp.maximum(largest, size)
    largest = jnp.maximum(largest, pltpu.roll(largest, LANES // 2, 1))
    scale = largest / math.sqrt(BLOCK) + 1e-05
    parity = (me ^ (me >> 1) ^ (me >> 2)) & 1
    sign = (1 - 2 * parity).astype(F32)
    for q in range(8):
        columns = slice(q * LANES, (q + 1) * LANES)
        rotated = hold[me * 8 + q] * sign / math.sqrt(BLOCK)
        scaled_ref[:, columns] = (rotated / scale).astype(BF16)
        scale_ref[:, columns] = scale


def unrotate_kernel(me_ref, *refs):
    *parts, out_ref = refs
    me = me_ref[0]
    row_count = parts[0].shape[0]
    total = None
    for d in range(8):
        both = (me ^ d) & me
        parity = (both ^ (both >> 1) ^ (both >> 2)) & 1
        sign = (1 - 2 * parity).astype(F32)
        tiles = [t * sign for t in block_tiles(parts, d, row_count)]
        total = tiles if total is None else [a + b for a, b in zip(total, tiles)]
    tiles = [lane_butterfly(t) for t in butterfly(total)]
    for q in range(8):
        out_ref[:, q * LANES : (q + 1) * LANES] = (tiles[q] / math.sqrt(BLOCK)).astype(BF16)


def dp_blocks(near):
    return near + [swap(jnp.concatenate(near, axis=0), "core", 1)]


def whole(shape):
    return pl.BlockSpec(shape, lambda i, me: (0, 0))


def rotate(parts, me):
    rows, width = parts[0].shape
    return pl.pallas_call(
        rotate_kernel,
        grid_spec=pltpu.PrefetchScalarGridSpec(
            num_scalar_prefetch=1,
            grid=(rows // 16,),
            in_specs=[whole(p.shape) for p in parts],
            out_specs=[pl.BlockSpec((16, width), lambda i, me: (i, 0))] * 2,
            scratch_shapes=[pltpu.VMEM((64, 16, LANES), F32)],
        ),
        out_shape=[
            jax.ShapeDtypeStruct((rows, width), BF16),
            jax.ShapeDtypeStruct((rows, width), F32),
        ],
        compiler_params=pltpu.CompilerParams(vmem_limit_bytes=24 * 1024 * 1024),
    )(me[None], *parts)


def unrotate(parts, me):
    rows, width = parts[0].shape
    return pl.pallas_call(
        unrotate_kernel,
        grid_spec=pltpu.PrefetchScalarGridSpec(
            num_scalar_prefetch=1,
            grid=(rows // 16,),
            in_specs=[whole(p.shape) for p in parts],
            out_specs=pl.BlockSpec((16, width), lambda i, me: (i, 0)),
        ),
        out_shape=jax.ShapeDtypeStruct((rows, width), BF16),
        compiler_params=pltpu.CompilerParams(vmem_limit_bytes=24 * 1024 * 1024),
    )(me[None], *parts)


def local(tokens, gate_weight, up_weight, down_weight, d_mixed):
    me = lax.axis_index("z") * 2 + lax.axis_index("core")
    hidden_share = gate_weight.shape[1]
    rows_first = (((0,), (0,)), ((), ()))
    weight_pair = jnp.concatenate([gate_weight, up_weight], axis=1)

    scaled, block_scale = rotate(dp_blocks(swaps(tokens, "z")), me)
    scaled = jnp.concatenate(swaps(scaled, "x"), axis=0)
    cot = jnp.concatenate(swaps(d_mixed, "y"), axis=0)
    scaled, cot = lax.optimization_barrier((scaled, cot))
    half = cot.shape[0] // 2
    one, three = swap(scaled, "y", 1), swap(scaled, "y", 3)
    cot_one, cot_three = swap(cot, "x", 1), swap(cot, "x", 3)
    first, second = three[:half], one[half:]
    scaled = [scaled, one, three, swap(first, "y", 1), swap(second, "y", 3)]
    cot_first = after(cot_three[:half], first, second)
    cot_second = after(cot_one[half:], first, second)
    cot = [cot, cot_one, cot_three, swap(cot_first, "x", 1), swap(cot_second, "x", 3)]

    scaled[0] = after(scaled[0], cot_first, cot_second)
    scaled_all = gather_place(scaled, "y")
    types = (BF16, BF16, BF16, F32)
    gate_up = core_sums(scaled_all, weight_pair, ((1,), (0,)), types)
    cot[0] = after(cot[0], gate_up[0])
    cot = gather_place(cot, "x")
    gate_up = send(gate_up[0], gate_up[1:], "z")
    hidden_grad = core_sums(cot, down_weight, ((1,), (1,)), types)
    hidden_grad = send(hidden_grad[0], hidden_grad[1:], "z")
    hidden, grad_pair = hidden_and_grads(gate_up, hidden_grad)

    hidden_pieces = swaps(hidden, "z")
    grad_one, grad_three = swap(grad_pair, "z", 1), swap(grad_pair, "z", 3)
    half = grad_pair.shape[0] // 2
    first, second = grad_three[:half], grad_one[half:]
    grad_pieces = [grad_pair, grad_one, grad_three, swap(first, "z", 1), swap(second, "z", 3)]
    hidden_pieces[0] = after(hidden_pieces[0], first, second)
    hidden_mine = gather_z(hidden_pieces)
    hidden_all = place_cores(hidden_mine, swap(hidden_mine, "core", 1))
    mixed = mixed_pieces(jnp.dot(hidden_all, down_weight, preferred_element_type=F32))
    mixed_received = relay_start(mixed, "x")

    grad_mine = gather_z([after(grad_pair, mixed[3])] + grad_pieces[1:])
    grad_other = swap(grad_mine, "core", 1)
    dims = (((1,), (1,)), ((), ()))
    partial = lax.dot_general(grad_mine, weight_pair, dims, preferred_element_type=F32)
    partial_other = lax.dot_general(
        after(grad_other, partial), weight_pair, dims, preferred_element_type=F32
    )
    pieces = scatter_pieces(partial, partial_other)
    received = relay_start(pieces, "y")
    mixed_received = [after(r, pieces[3]) for r in mixed_received]
    mixed_middle = relay_middle(mixed, mixed_received)
    mixed_received = relay_end(mixed_middle, "x")
    received = [after(r, *mixed_middle) for r in received]
    middle = relay_middle(pieces, received)
    received = relay_end(middle, "y")
    mixed = mixed_last(summed((after(mixed[0], *middle), mixed_received)))
    mixed_received = send(mixed[0], mixed[1:], "y")[1]
    grad_all = place_cores(after(grad_mine, *mixed[1:]), grad_other)
    grad_gate = lax.dot_general(
        scaled_all, grad_all[:, :hidden_share], rows_first, preferred_element_type=F32
    )
    own = after(pieces[0], grad_gate, *mixed_received)
    last = scatter_last(summed((own, received)))
    received = send(last[0], last[1:], "x")[1]
    grad_up = lax.dot_general(
        after(scaled_all, *last[1:]),
        grad_all[:, hidden_share:],
        rows_first,
        preferred_element_type=F32,
    )
    scaled_grad = summed((after(last[0], grad_up), received))
    unscaled = (scaled_grad / block_scale).astype(BF16)
    near = swaps(unscaled, "z")
    mixed = summed((after(mixed[0], unscaled), mixed_received)).astype(BF16)
    grad_down = lax.dot_general(
        after(hidden_all, unscaled), cot, rows_first, preferred_element_type=F32
    )
    d_tokens = unrotate(dp_blocks([after(near[0], grad_down)] + near[1:]), me)
    return (mixed, d_tokens, grad_gate, grad_up, grad_down)


def solution(mesh):
    split = Mesh(mesh.devices.reshape(4, 2, 4, 4), ("z", "core", "y", "x"))
    tokens = P(("y", "x"), ("z", "core"))
    weight = P(("z", "core"), ("y", "x"))
    down = P(("y", "x"), ("z", "core"))
    return jax.shard_map(
        local,
        mesh=split,
        in_specs=(tokens, weight, weight, down, tokens),
        out_specs=(tokens, tokens, weight, weight, down),
        check_vma=False,
    )
```
